1024 devices in a mesh: node: 256 (over x, z_lo, y), local: 4 (over z_hi, core).
Axes of the slice: x: 8, y: 8, z: 8 (z_hi: 2, z_lo: 4; z = z_hi * 4 + z_lo), core: 2. Of those that a mesh axis runs over, the one named last changes fastest.
Arguments:
- x_groups: bfloat16 [65536, 2560], P('node'), may hold values from -6 to 6
- group_len: int32 [256, 4, 2], replicated, may hold values from 10 to 32, as said below
- act_grad: bfloat16 [65536, 1024], P('node', 'local'), may hold values from -24 to 24
- slot_gate: bfloat16 [65536], P('node'), may hold values from 0.099609375 to 1
- gate_up: bfloat16 [256, 2560, 1024], P('node', None, 'local'), may hold values from -0.125 to 0.125
Outputs:
- grad_rows: bfloat16 [65536, 2560], P(('node', 'local'))
- grad_gate_up: bfloat16 [256, 2560, 1024], P('node', None, 'local')
The draws below stay inside these ranges and needn't reach their ends.
Inputs may be any that keep to these rules, and one draw needn't show every extreme that they name: `group_len`: in each of the two groups some device has all 32 slots live.
All inputs are finite; a program needn't handle non-finite values.
Results may differ from the reference program's by a relative error of at most 0.015.
Values may be sent and summed in bfloat16 or wider, within the bound.
No kernel may reach another device: no remote copies, remote signals or barrier semaphores. Data moves between devices by JAX's collectives and lax.ppermute only.
A program may use at most 32 MiB of HBM per device.

```python
import math
import jax
import jax.numpy as jnp
from jax import lax

D = 2560
H = 1024
CAP = 32
SLOTS = 65536
N_NODE = 256
N_LOCAL = 4


def draw_group_len(key, part):
    key = jax.random.fold_in(key, 11)
    first, second = jax.random.split(key)
    lengths = jax.random.randint(first, (N_NODE * N_LOCAL, 2), max(1, CAP // 3), CAP + 1)
    chosen = jax.random.randint(second, (2,), 0, N_NODE * N_LOCAL)
    lengths = jnp.where(jnp.arange(N_NODE * N_LOCAL)[:, None] == chosen[None, :], CAP, lengths)
    return lengths.reshape(N_NODE, N_LOCAL, 2).astype(jnp.int32)


def block_levels(rng, dims, pieces, smallest, high):
    gain = 1.0
    for axis_at, parts in pieces:
        steps = jax.random.uniform(jax.random.fold_in(jax.random.fold_in(rng, 6), axis_at), (parts,), jnp.float32, smallest / len(pieces), high / len(pieces))
        gain = gain * jnp.repeat(jnp.exp(steps), dims[axis_at] // parts).reshape((-1,) + (1,) * (len(dims) - 1 - axis_at))
    return gain


def bell_draw(rng, shape, width, limit, shards=(), dtype=jnp.bfloat16):
    level = block_levels(rng, shape, shards, -0.22, 0.18) if shards else 1.0
    entries = jax.random.normal(rng, shape, jnp.float32) * width * level
    return jnp.minimum(jnp.maximum(entries, -limit), limit).astype(dtype)


def setup_inputs(seed: int = 0) -> dict:
    key_list = jax.random.split(jax.random.key(seed), 6)
    x_groups = bell_draw(key_list[0], (SLOTS, D), 1.0, 6.0, ((0, 256),))
    group_len = draw_group_len(jax.random.fold_in(key_list[5], 71), 0)
    act_grad = bell_draw(key_list[2], (SLOTS, H), 4.0, 24.0, ((0, 256), (1, 4)))
    slot_gate = jnp.clip(jnp.exp(math.log(1.0) - 2.306499 * jax.random.uniform(key_list[3], (SLOTS,), jnp.float32) ** block_levels(key_list[3], (SLOTS,), ((0, 256),), -0.2, 0.2)), 0.099609375, 1.0).astype(jnp.bfloat16)
    gate_up = bell_draw(key_list[4], (N_NODE, D, H), D ** -0.5, 0.125, ((0, 256), (2, 4)))
    return {"x_groups": x_groups, "group_len": group_len, "act_grad": act_grad, "slot_gate": slot_gate, "gate_up": gate_up}


def expert_work(slot_rows, cotangents, gate_values, w_gate, w_up, factor, block_width, block_count):
    gate_part = jnp.dot(slot_rows, w_gate, preferred_element_type=jnp.float32)
    up_part = jnp.dot(slot_rows, w_up, preferred_element_type=jnp.float32)
    weighted = gate_values.astype(jnp.float32)[:, None] * cotangents.astype(jnp.float32)
    sigmoid_g = jax.nn.sigmoid(gate_part)
    d_gate = (weighted * up_part * sigmoid_g * (1.0 + gate_part * (1.0 - sigmoid_g))).astype(jnp.bfloat16)
    d_up = (weighted * gate_part * sigmoid_g).astype(jnp.bfloat16)
    summed = jnp.zeros((slot_rows.shape[0], slot_rows.shape[1]), jnp.float32)
    for column_block in range(block_count):
        first_col = column_block * block_width
        last_col = first_col + block_width
        partial_value = jnp.dot(d_gate[:, first_col:last_col], w_gate[:, first_col:last_col].T, preferred_element_type=jnp.float32)
        partial_value = partial_value + jnp.dot(d_up[:, first_col:last_col], w_up[:, first_col:last_col].T, preferred_element_type=jnp.float32)
        summed = summed + lax.optimization_barrier(partial_value.astype(jnp.bfloat16)).astype(jnp.float32)
    term_gate = jnp.dot(slot_rows.T, d_gate, preferred_element_type=jnp.float32) * factor
    term_up = jnp.dot(slot_rows.T, d_up, preferred_element_type=jnp.float32) * factor
    return (summed.astype(jnp.bfloat16), term_gate, term_up)

def reference(x_groups, group_len, act_grad, slot_gate, gate_up):
    experts = N_NODE // 2
    block_width = H // (2 * N_LOCAL)
    block_count = 2 * N_LOCAL
    factor = 1.0 / math.sqrt(4 * N_LOCAL * CAP)
    pair_count = 2 * N_LOCAL * CAP
    alive = jnp.arange(CAP)[None, None, None, :] < group_len[:, :, :, None]
    x_slots = x_groups.reshape(N_NODE, N_LOCAL, 2, CAP, D)
    x_slots = jnp.where(alive[:, :, :, :, None], x_slots, jnp.zeros_like(x_slots))
    a_slots = act_grad.reshape(N_NODE, N_LOCAL, 2, CAP, H)
    g_slots = slot_gate.reshape(N_NODE, N_LOCAL, 2, CAP)

    def by_group(array, group, tail):
        return array[:, :, group].reshape((experts, pair_count) + tail)
    own_x = by_group(x_slots, 0, (D,))
    own_a = by_group(a_slots, 0, (H,))
    own_g = by_group(g_slots, 0, ())
    prev_x = jnp.roll(by_group(x_slots, 1, (D,)), 1, axis=0)
    prev_a = jnp.roll(by_group(a_slots, 1, (H,)), 1, axis=0)
    prev_g = jnp.roll(by_group(g_slots, 1, ()), 1, axis=0)
    weights = gate_up.reshape(experts, 2, D, N_LOCAL, 2, block_width)

    def one_expert(carry, items):
        held, own_rows, own_cot, own_gate, prev_rows, prev_cot, prev_gate = items
        w_gate = jnp.transpose(held[:, :, :, 0, :], (1, 2, 0, 3)).reshape(D, H)
        w_up = jnp.transpose(held[:, :, :, 1, :], (1, 2, 0, 3)).reshape(D, H)
        own_dx, own_tg, own_tu = expert_work(own_rows, own_cot, own_gate, w_gate, w_up, factor, block_width, block_count)
        prev_dx, prev_tg, prev_tu = expert_work(prev_rows, prev_cot, prev_gate, w_gate, w_up, factor, block_width, block_count)
        from_gate = lax.optimization_barrier(prev_tg.astype(jnp.bfloat16)).astype(jnp.float32)
        from_up = lax.optimization_barrier(prev_tu.astype(jnp.bfloat16)).astype(jnp.float32)
        grad_gate = (own_tg + from_gate).reshape(D, N_LOCAL, 2, block_width)
        grad_up = (own_tu + from_up).reshape(D, N_LOCAL, 2, block_width)
        joined = jnp.stack([grad_gate, grad_up], axis=3)
        joined = jnp.transpose(joined, (2, 0, 1, 3, 4)).reshape(2, D, H)
        return (carry, (joined.astype(jnp.bfloat16), own_dx, prev_dx))
    start_carry = jnp.zeros((), jnp.float32)
    unused, outputs = lax.scan(one_expert, start_carry, (weights, own_x, own_a, own_g, prev_x, prev_a, prev_g))
    grads, own_dx, prev_dx = outputs
    first_rows = own_dx.reshape(N_NODE, N_LOCAL, CAP, D)
    second_rows = jnp.roll(prev_dx, -1, axis=0).reshape(N_NODE, N_LOCAL, CAP, D)
    all_rows = jnp.stack([first_rows, second_rows], axis=2)
    all_rows = jnp.where(alive[:, :, :, :, None], all_rows, jnp.zeros_like(all_rows))
    return (all_rows.reshape(SLOTS, D), grads.reshape(N_NODE, D, H))
```

```python
import math

import jax
import jax.numpy as jnp
from jax import lax
from jax.sharding import PartitionSpec as P

BF = jnp.bfloat16
F32 = jnp.float32


def ahead(value, steps):
    count = lax.axis_size("node")
    return lax.ppermute(value, "node", [(i, (i + steps) % count) for i in range(count)])


def swapped(value, axis, bit):
    count = lax.axis_size(axis)
    return lax.ppermute(value, axis, [(i, i ^ (1 << bit)) for i in range(count)])


def pick(array, index, axis):
    return lax.dynamic_index_in_dim(array, index, axis, keepdims=False)


def hidden_grads(rows, cot, weights, width):
    hidden = jnp.dot(rows, weights, preferred_element_type=F32)
    parts = []
    for k in range(2):
        gate = hidden[:, 2 * k * width : (2 * k + 1) * width]
        up = hidden[:, (2 * k + 1) * width : (2 * k + 2) * width]
        c = cot[:, k * width : (k + 1) * width].astype(F32)
        s = jax.nn.sigmoid(gate)
        parts += [c * up * s * (1.0 + gate * (1.0 - s)), c * gate * s]
    return jnp.concatenate(parts, axis=1).astype(BF)


def row_grads(dh, weights):
    return lax.dot_general(dh, weights, (((1,), (1,)), ((), ())), preferred_element_type=F32)


def weight_grads(rows, dh):
    return lax.dot_general(rows, dh, (((0,), (0,)), ((), ())), preferred_element_type=F32)


def on_device(x_groups, group_len, act_grad, slot_gate, gate_up):
    node_rows, dim = x_groups.shape
    in_node = lax.axis_size("local")
    cap = node_rows // (2 * in_node)
    width = gate_up.shape[2] // 2
    half = in_node // 2 * cap
    node = lax.axis_index("node")
    local = lax.axis_index("local")
    core = local % 2
    far = local // 2
    parity = node % 2
    factor = 1.0 / math.sqrt(4 * in_node * cap)

    own_w = gate_up[0]
    acts = act_grad.reshape(in_node // 2, 2, 2, cap, 2 * width)
    act_other = swapped(pick(acts, 1 - core, 1), "local", 0)
    act_mine = pick(acts, core, 1)
    both_w = jnp.concatenate([own_w, swapped(own_w, "local", 0)], axis=1)

    lengths = pick(group_len, node, 0)
    alive = jnp.arange(cap)[None, None, :] < lengths[:, :, None]
    alive_half = pick(alive.reshape(in_node // 2, 2, 2, cap), core, 1)
    rows = pick(x_groups.reshape(in_node // 2, 2, 2, cap, dim), core, 1)
    rows = jnp.where(alive_half[..., None], rows, jnp.zeros_like(rows))
    gates = pick(slot_gate.reshape(in_node // 2, 2, 2, cap), core, 1).astype(F32)

    def cots(which):
        cut = [
            pick(a.reshape(in_node // 2, 2, cap, 2, width), which, 3) for a in (act_mine, act_other)
        ]
        both = jnp.concatenate(cut, axis=-1).astype(F32)
        return (both * gates[..., None]).astype(BF)

    keep = cots(parity)
    give = cots(1 - parity)

    def group(array, k):
        return array[:, k].reshape(half, array.shape[-1])

    sent1 = ahead(jnp.concatenate([group(rows, 1), group(give, 1), group(keep, 1)], axis=1), 2)
    sent0 = jnp.concatenate([group(rows, 0), group(give, 0)], axis=1)
    got0 = swapped(sent0, "node", 0)
    got1 = swapped(sent1[:, : dim + 2 * width], "node", 0)

    rows0 = jnp.concatenate([group(rows, 0), got0[:, :dim]], axis=0)
    cot0 = jnp.concatenate([group(keep, 0), got0[:, dim:]], axis=0)
    rows1 = jnp.concatenate([sent1[:, :dim], got1[:, :dim]], axis=0)
    cot1 = jnp.concatenate([sent1[:, dim + 2 * width :], got1[:, dim:]], axis=0)

    def summed(dx):
        own = dx[:half] + swapped(dx[half:].astype(BF), "node", 0).astype(F32)
        own = own.reshape(2, cap, dim)
        away = swapped(pick(own, 1 - far, 0).astype(BF), "local", 1).astype(F32)
        return (pick(own, far, 0) + away).astype(BF)

    dh0 = hidden_grads(rows0, cot0, both_w, width)
    out0 = summed(row_grads(dh0, both_w))
    dh1 = hidden_grads(rows1, cot1, both_w, width)
    out1 = ahead(summed(row_grads(dh1, both_w)), -2)

    all_rows = jnp.concatenate([rows0, rows1], axis=0)
    all_dh = jnp.concatenate([dh0, dh1], axis=0)
    other_dw = (weight_grads(all_rows, all_dh[:, 2 * width :]) * factor).astype(BF)
    other_dw = swapped(other_dw, "local", 0)
    own_dw = weight_grads(all_rows, all_dh[:, : 2 * width]) * factor
    grad_weights = (own_dw + other_dw.astype(F32)).astype(BF)

    mine = pick(alive, local, 0)
    finished = jnp.stack([out0, out1], axis=0)
    finished = jnp.where(mine[:, :, None], finished, jnp.zeros_like(finished))
    return (finished.reshape(2 * cap, dim), grad_weights[None])


def solution(mesh):
    placed = (P("node", None), P(), P("node", "local"), P("node"), P("node", None, "local"))
    return jax.shard_map(
        on_device,
        mesh=mesh,
        in_specs=placed,
        out_specs=(P(("node", "local"), None), P("node", None, "local")),
        check_vma=False,
    )
```

```python
import math

import jax
import jax.numpy as jnp
from jax import lax
from jax.experimental import pallas as pl
from jax.experimental.pallas import tpu as pltpu
from jax.sharding import PartitionSpec as P

BF = jnp.bfloat16
F32 = jnp.float32


def moved(value, node_step, node_flip, local_flip):
    nodes, in_node = lax.axis_size("node"), lax.axis_size("local")
    route = []
    for n in range(nodes):
        for l in range(in_node):
            target = ((n + node_step) % nodes) ^ node_flip
            route.append((n * in_node + l, target * in_node + (l ^ local_flip)))
    return lax.ppermute(value, ("node", "local"), route)


def pick(array, index, axis):
    return lax.dynamic_index_in_dim(array, index, axis, keepdims=False)


def expert_kernel(own_ref, own_cot_ref, got_ref, got_cot_ref, own_w_ref, other_w_ref, dh_ref, give_ref, keep_ref):
    half, dim = keep_ref.shape
    width = own_w_ref.shape[1] // 2
    x = jnp.concatenate([own_ref[:, :dim], got_ref[:, :dim]], axis=0)
    cot = jnp.concatenate([own_cot_ref[...], got_cot_ref[...]], axis=0)
    weights = (own_w_ref, other_w_ref)
    dhs = []
    for k in range(2):
        hidden = jnp.dot(x, weights[k][...], preferred_element_type=F32)
        gate = hidden[:, :width]
        up = hidden[:, width:]
        c = cot[:, k * width : (k + 1) * width].astype(F32)
        s = jax.nn.sigmoid(gate)
        cs = c * s
        dh = jnp.concatenate([cs * up * (1.0 + gate * (1.0 - s)), cs * gate], axis=1).astype(BF)
        dh_ref[:, 2 * k * width : 2 * (k + 1) * width] = dh
        dhs.append(dh)
    step = 512
    for first in range(0, dim, step):
        total = None
        for k in range(2):
            part = lax.dot_general(
                dhs[k],
                weights[k][first : first + step, :],
                (((1,), (1,)), ((), ())),
                preferred_element_type=F32,
            )
            total = part if total is None else total + part
        keep_ref[:, first : first + step] = total[:half]
        give_ref[:, first : first + step] = total[half:].astype(BF)


def expert_work(own, own_cot, got, got_cot, own_w, other_w):
    half = own.shape[0]
    dim, wide = own_w.shape
    vmem = pl.BlockSpec(memory_space=pltpu.VMEM)
    return pl.pallas_call(
        expert_kernel,
        out_shape=(
            jax.ShapeDtypeStruct((2 * half, 2 * wide), BF),
            jax.ShapeDtypeStruct((half, dim), BF),
            jax.ShapeDtypeStruct((half, dim), F32),
        ),
        in_specs=[vmem] * 6,
        out_specs=(vmem,) * 3,
        compiler_params=pltpu.CompilerParams(vmem_limit_bytes=32 * 1024 * 1024),
        cost_estimate=pl.CostEstimate(
            flops=8 * half * dim * wide * 2, bytes_accessed=8 * 1024 * 1024, transcendentals=2 * half * wide
        ),
    )(own, own_cot, got, got_cot, own_w, other_w)


def weight_grads(rows, dh):
    return lax.dot_general(rows, dh, (((0,), (0,)), ((), ())), preferred_element_type=F32)


def on_device(x_groups, group_len, act_grad, slot_gate, gate_up):
    node_rows, dim = x_groups.shape
    in_node = lax.axis_size("local")
    far_count = in_node // 2
    cap = node_rows // (2 * in_node)
    width = gate_up.shape[2] // 2
    half = far_count * cap
    node = lax.axis_index("node")
    local = lax.axis_index("local")
    core = local % 2
    far = local // 2
    parity = node % 2
    factor = 1.0 / math.sqrt(4 * in_node * cap)

    own_w = gate_up[0]

    def rows_of(array, k):
        shaped = array.reshape(far_count, 2, 2, cap, dim)
        return lax.dynamic_slice(
            shaped, (0, core, k, 0, 0), (far_count, 1, 1, cap, dim)
        ).reshape(half, dim)

    rows1 = rows_of(x_groups, 1)
    rows1, act_grad, x_groups, own_w = lax.optimization_barrier((rows1, act_grad, x_groups, own_w))
    own1 = moved(rows1, 2, 0, 0)

    acts = act_grad.reshape(far_count, 2, 2, cap, 2 * width)
    act_other = moved(pick(acts, 1 - core, 1), 0, 0, 1)
    act_mine = pick(acts, core, 1)
    lengths = pick(group_len, node, 0)
    alive = jnp.arange(cap)[None, None, :] < lengths[:, :, None]
    gates = jnp.where(alive.reshape(node_rows), slot_gate, jnp.zeros_like(slot_gate))
    gates = pick(gates.reshape(far_count, 2, 2, cap), core, 1).astype(F32)

    def cots(which):
        cut_to = [
            pick(a.reshape(far_count, 2, cap, 2, width), which, 3) for a in (act_mine, act_other)
        ]
        both = jnp.concatenate(cut_to, axis=-1).astype(F32)
        return (both * gates[..., None]).astype(BF)

    def group(array, k):
        return array[:, k].reshape(half, array.shape[-1])

    keep = cots(parity)
    give = cots(1 - parity)
    own0 = jnp.concatenate([rows_of(x_groups, 0), group(give, 0)], axis=1)
    got0 = moved(own0, 0, 1, 0)
    other_w = moved(own_w, 0, 0, 1)
    cots1 = moved(jnp.concatenate([group(give, 1), group(keep, 1)], axis=1), 2, 0, 0)

    got1 = moved(jnp.concatenate([own1, cots1[:, : 2 * width]], axis=1), 0, 1, 0)
    dh0, send0, kept0 = expert_work(own0, group(keep, 0), got0, got0[:, dim:], own_w, other_w)
    got1, _ = lax.optimization_barrier((got1, kept0))
    back0 = moved(send0, 0, 1, 0)
    dh1, send1, kept1 = expert_work(own1, cots1[:, 2 * width :], got1, got1[:, dim:], own_w, other_w)
    back1 = moved(send1, 0, 1, 0)

    all_rows = [own0[:, :dim], got0[:, :dim], own1, got1[:, :dim]]
    all_rows = jnp.concatenate(all_rows, axis=0)
    all_dh = jnp.concatenate([dh0, dh1], axis=0)
    other_dw = (weight_grads(all_rows, all_dh[:, 2 * width :]) * factor).astype(BF)
    other_dw = moved(other_dw, 0, 0, 1)

    sum1 = (kept1 + back1.astype(F32)).reshape(far_count, cap, dim)
    _, back0 = lax.optimization_barrier((sum1, back0))
    away1 = moved(pick(sum1, 1 - far, 0).astype(BF), 0, 0, 2)
    sum0 = (kept0 + back0.astype(F32)).reshape(far_count, cap, dim)
    away0 = moved(pick(sum0, 1 - far, 0).astype(BF), 0, 0, 2)
    out1 = (pick(sum1, far, 0) + away1.astype(F32)).astype(BF)
    out1 = moved(out1, -2, 0, 0)
    out0 = pick(sum0, far, 0) + away0.astype(F32)

    own_dw = weight_grads(all_rows, all_dh[:, : 2 * width]) * factor
    grad_weights = (own_dw + other_dw.astype(F32)).astype(BF)
    out1, grad_weights = lax.optimization_barrier((out1, grad_weights))

    mine = pick(alive, local, 0)
    finished = jnp.stack([out0, out1.astype(F32)], axis=0)
    finished = jnp.where(mine[:, :, None], finished, jnp.zeros_like(finished)).astype(BF)
    return (finished.reshape(2 * cap, dim), grad_weights[None])


def solution(mesh):
    placed = (P("node", None), P(), P("node", "local"), P("node"), P("node", None, "local"))
    return jax.shard_map(
        on_device,
        mesh=mesh,
        in_specs=placed,
        out_specs=(P(("node", "local"), None), P("node", None, "local")),
        check_vma=False,
    )
```

```python
import math

import jax
import jax.numpy as jnp
from jax import lax
from jax.experimental import pallas as pl
from jax.experimental.pallas import tpu as pltpu
from jax.sharding import PartitionSpec as P

BF = jnp.bfloat16
F32 = jnp.float32


def moved(value, node_step, node_flip, local_flip):
    nodes, in_node = lax.axis_size("node"), lax.axis_size("local")
    route = []
    for n in range(nodes):
        for l in range(in_node):
            target = ((n + node_step) % nodes) ^ node_flip
            route.append((n * in_node + l, target * in_node + (l ^ local_flip)))
    return lax.ppermute(value, ("node", "local"), route)


def pick(array, index, axis):
    return lax.dynamic_index_in_dim(array, index, axis, keepdims=False)


def gate_kernel(len_ref, gate_ref, out_ref, column_ref):
    count = gate_ref.shape[1]
    cap = count // 8
    core = lax.rem(lax.axis_index("local"), 2)
    shape = (count, count)
    diagonal = lax.broadcasted_iota(jnp.int32, shape, 0) == lax.broadcasted_iota(jnp.int32, shape, 1)
    gate = jnp.broadcast_to(gate_ref[...].astype(F32), shape)
    column = jnp.sum(jnp.where(diagonal, gate, 0.0), axis=1, keepdims=True)
    column_ref[...] = jnp.broadcast_to(column, column_ref.shape)
    slot = lax.broadcasted_iota(jnp.int32, (cap, out_ref.shape[1]), 0)
    for chip in range(2):
        for k in range(2):
            block = (2 * chip + core) * 2 + k
            gates = column_ref[pl.ds(pl.multiple_of(block * cap, cap), cap), :]
            first = (2 * chip + k) * cap
            out_ref[first : first + cap, :] = jnp.where(slot < len_ref[block], gates, 0.0)


def live_gates(lengths, gates, wide):
    count = gates.shape[1]
    vmem = pl.BlockSpec(memory_space=pltpu.VMEM)
    return pl.pallas_call(
        gate_kernel,
        out_shape=jax.ShapeDtypeStruct((count // 2, wide), F32),
        in_specs=[pl.BlockSpec(memory_space=pltpu.SMEM), vmem],
        out_specs=vmem,
        scratch_shapes=[pltpu.VMEM((count, wide), F32)],
        compiler_params=pltpu.CompilerParams(vmem_limit_bytes=4 * 1024 * 1024),
        cost_estimate=pl.CostEstimate(
            flops=8 * count * count, bytes_accessed=64 * 1024 * 1024, transcendentals=0
        ),
    )(lengths, gates)


def expert_kernel(own_ref, own_cot_ref, got_ref, got_cot_ref, own_w_ref, other_w_ref, dh_ref, give_ref, keep_ref):
    half, dim = keep_ref.shape
    width = own_w_ref.shape[1] // 2
    x = jnp.concatenate([own_ref[:, :dim], got_ref[:, :dim]], axis=0)
    cot = jnp.concatenate([own_cot_ref[...], got_cot_ref[...]], axis=0)
    weights = (own_w_ref, other_w_ref)
    dhs = []
    for k in range(2):
        hidden = jnp.dot(x, weights[k][...], preferred_element_type=F32)
        gate = hidden[:, :width]
        up = hidden[:, width:]
        c = cot[:, k * width : (k + 1) * width].astype(F32)
        s = jax.nn.sigmoid(gate)
        cs = c * s
        dh = jnp.concatenate([cs * up * (1.0 + gate * (1.0 - s)), cs * gate], axis=1).astype(BF)
        dh_ref[:, 2 * k * width : 2 * (k + 1) * width] = dh
        dhs.append(dh)
    step = 512
    for first in range(0, dim, step):
        total = None
        for k in range(2):
            part = lax.dot_general(
                dhs[k],
                weights[k][first : first + step, :],
                (((1,), (1,)), ((), ())),
                preferred_element_type=F32,
            )
            total = part if total is None else total + part
        keep_ref[:, first : first + step] = total[:half]
        give_ref[:, first : first + step] = total[half:].astype(BF)


def expert_work(own, own_cot, got, got_cot, own_w, other_w):
    half = own.shape[0]
    dim, wide = own_w.shape
    vmem = pl.BlockSpec(memory_space=pltpu.VMEM)
    return pl.pallas_call(
        expert_kernel,
        out_shape=(
            jax.ShapeDtypeStruct((2 * half, 2 * wide), BF),
            jax.ShapeDtypeStruct((half, dim), BF),
            jax.ShapeDtypeStruct((half, dim), F32),
        ),
        in_specs=[vmem] * 6,
        out_specs=(vmem,) * 3,
        compiler_params=pltpu.CompilerParams(vmem_limit_bytes=12 * 1024 * 1024),
        cost_estimate=pl.CostEstimate(
            flops=16 * half * dim * wide, bytes_accessed=4 * 1024 * 1024, transcendentals=2 * half * wide
        ),
    )(own, own_cot, got, got_cot, own_w, other_w)


def weight_grads(rows, dh):
    return lax.dot_general(rows, dh, (((0,), (0,)), ((), ())), preferred_element_type=F32)


def on_device(x_groups, group_len, act_grad, slot_gate, gate_up):
    node_rows, dim = x_groups.shape
    in_node = lax.axis_size("local")
    far_count = in_node // 2
    cap = node_rows // (2 * in_node)
    width = gate_up.shape[2] // 2
    half = far_count * cap
    node = lax.axis_index("node")
    local = lax.axis_index("local")
    core = local % 2
    far = local // 2
    parity = node % 2
    factor = 1.0 / math.sqrt(4 * in_node * cap)

    own_w = gate_up[0]

    def rows_of(array, k):
        shaped = array.reshape(far_count, 2, 2, cap, dim)
        return lax.dynamic_slice(
            shaped, (0, core, k, 0, 0), (far_count, 1, 1, cap, dim)
        ).reshape(half, dim)

    rows1 = rows_of(x_groups, 1)
    rows1, act_grad, x_groups, own_w = lax.optimization_barrier((rows1, act_grad, x_groups, own_w))
    own1 = moved(rows1, 2, 0, 0)

    acts = act_grad.reshape(far_count, 2, 2, cap, 2 * width)
    act_other = moved(pick(acts, 1 - core, 1), 0, 0, 1)
    act_mine = pick(acts, core, 1)
    lengths = pick(group_len, node, 0)
    alive = jnp.arange(cap)[None, None, :] < lengths[:, :, None]
    gates = live_gates(lengths.reshape(-1), slot_gate.reshape(1, node_rows), 2 * width)
    gates = gates.reshape(far_count, 2, cap, 2 * width)

    def cots(which):
        cut_to = [
            pick(a.reshape(far_count, 2, cap, 2, width), which, 3) for a in (act_mine, act_other)
        ]
        both = jnp.concatenate(cut_to, axis=-1).astype(F32)
        return (both * gates).astype(BF)

    def group(array, k):
        return array[:, k].reshape(half, array.shape[-1])

    keep = cots(parity)
    give = cots(1 - parity)
    own0 = jnp.concatenate([rows_of(x_groups, 0), group(give, 0)], axis=1)
    got0 = moved(own0, 0, 1, 0)
    other_w = moved(own_w, 0, 0, 1)
    cots1 = moved(jnp.concatenate([group(give, 1), group(keep, 1)], axis=1), 2, 0, 0)

    got1 = moved(jnp.concatenate([own1, cots1[:, : 2 * width]], axis=1), 0, 1, 0)
    dh0, send0, kept0 = expert_work(own0, group(keep, 0), got0, got0[:, dim:], own_w, other_w)
    got1, _ = lax.optimization_barrier((got1, kept0))
    back0 = moved(send0, 0, 1, 0)
    dh1, send1, kept1 = expert_work(own1, cots1[:, 2 * width :], got1, got1[:, dim:], own_w, other_w)
    back1 = moved(send1, 0, 1, 0)

    all_rows = [own0[:, :dim], got0[:, :dim], own1, got1[:, :dim]]
    all_rows = jnp.concatenate(all_rows, axis=0)
    all_dh = jnp.concatenate([dh0, dh1], axis=0)
    other_dw = (weight_grads(all_rows, all_dh[:, 2 * width :]) * factor).astype(BF)
    other_dw = moved(other_dw, 0, 0, 1)

    sum1 = (kept1 + back1.astype(F32)).reshape(far_count, cap, dim)
    _, back0 = lax.optimization_barrier((sum1, back0))
    away1 = moved(pick(sum1, 1 - far, 0).astype(BF), 0, 0, 2)
    sum0 = (kept0 + back0.astype(F32)).reshape(far_count, cap, dim)
    away0 = moved(pick(sum0, 1 - far, 0).astype(BF), 0, 0, 2)
    out1 = (pick(sum1, far, 0) + away1.astype(F32)).astype(BF)
    out1 = moved(out1, -2, 0, 0)
    out0 = pick(sum0, far, 0) + away0.astype(F32)

    own_dw = weight_grads(all_rows, all_dh[:, : 2 * width]) * factor
    grad_weights = (own_dw + other_dw.astype(F32)).astype(BF)
    out1, grad_weights = lax.optimization_barrier((out1, grad_weights))

    mine = pick(alive, local, 0)
    finished = jnp.stack([out0, out1.astype(F32)], axis=0)
    finished = jnp.where(mine[:, :, None], finished, jnp.zeros_like(finished)).astype(BF)
    return (finished.reshape(2 * cap, dim), grad_weights[None])


def solution(mesh):
    placed = (P("node", None), P(), P("node", "local"), P("node"), P("node", None, "local"))
    return jax.shard_map(
        on_device,
        mesh=mesh,
        in_specs=placed,
        out_specs=(P(("node", "local"), None), P("node", None, "local")),
        check_vma=False,
    )
```
